512 devices in a mesh: seq: 16 (over y_lo, z), exp: 32 (over x, y_hi, core).
Axes of the slice: x: 4, y: 8 (y_hi: 4, y_lo: 2; y = y_hi * 2 + y_lo), z: 8, core: 2. Of those that a mesh axis runs over, the one named last changes fastest.
Arguments:
- resid: bfloat16 [32, 2048, 2048], P('exp', 'seq'), may hold values from -60 to 60
- norm_gain: float32 [2048], replicated, may hold values from 0.1 to 1.9
- router_logits: float32 [32, 2048, 32], P('exp', 'seq'), may hold values from -20 to 280
- router_weight: bfloat16 [2048, 32], replicated, may hold values from -0.125 to 0.125
- expert_index: int32 [32, 2048], P('exp', 'seq'), may hold values from 0 to 31, as said below
- slot: int32 [32, 2048], P('exp', 'seq'), may hold values from 0 to 3, as said below
- w_in: bfloat16 [32, 2048, 5120], P('exp', None, 'seq'), may hold values from -0.125 to 0.125
- w_out: bfloat16 [32, 5120, 2048], P('exp', 'seq'), may hold values from -0.078125 to 0.078125
- grad_out: bfloat16 [32, 2048, 2048], P('exp', 'seq'), may hold values from -6 to 6
- queries: bfloat16 [32, 2048, 2048], P('exp', 'seq'), may hold values from -6 to 6
- keys: bfloat16 [32, 64, 2048], P('exp', None, 'seq'), may hold values from -6 to 6
- values: bfloat16 [32, 64, 2048], P('exp', None, 'seq'), may hold values from -6 to 6
Outputs:
- grad_stream: bfloat16 [32, 2048, 2048], P('exp', 'seq')
- grad_keys: bfloat16 [32, 64, 2048], P('exp', None, 'seq')
- grad_values: bfloat16 [32, 64, 2048], P('exp', None, 'seq')
The draws below stay inside these ranges and needn't reach their ends.
Inputs may be any that keep to these rules, and one draw needn't show every extreme that they name: `expert_index`: in every block of 128 tokens one expert, the same in all blocks, is named by more than 3 tokens. A token's slot is the number of earlier tokens of its block with the same expert_index, or 3 where that number is 3 or more.
All inputs are finite; a program needn't handle non-finite values.
Results may differ from the reference program's by a relative error of at most 0.018.
Values may be sent and summed in bfloat16 or wider, within the bound.
No kernel may reach another device: no remote copies, remote signals or barrier semaphores. Data moves between devices by JAX's collectives and lax.ppermute only.
A program may use at most 128 MiB of HBM per device.

```python
import jax
import jax.numpy as jnp
from jax import lax

D = 2048
HEADS = 32
HEAD_DIM = 64
FF = 5120
TOK_DEV = 128
ENC = 64
EXPERTS = 32
HID = 320
CAP = 3
DEC = 2048
DOCS = 32
N_SEQ = 16


def routing(key):
    blocks = DOCS * (DEC // TOK_DEV)
    key_a, key_b, key_c, key_d = jax.random.split(key, 4)
    first = jax.random.randint(key_a, (blocks, TOK_DEV), 0, EXPERTS)
    second = jax.random.randint(key_b, (blocks, TOK_DEV), 0, EXPERTS)
    ranking = jax.random.permutation(key_c, EXPERTS)
    chosen = ranking[jnp.minimum(first, second)]
    scores = jax.random.randint(key_d, (blocks, TOK_DEV), 0, 1 << 20) * TOK_DEV + jnp.arange(TOK_DEV, dtype=jnp.int32)[None, :]
    order = jnp.argsort(jnp.argsort(scores, axis=1), axis=1)
    chosen = jnp.where(order <= CAP, ranking[0], chosen)
    onehot = (chosen[:, :, None] == jnp.arange(EXPERTS, dtype=jnp.int32)[None, None, :]).astype(jnp.int32)
    earlier = jnp.cumsum(onehot, axis=1) - onehot
    slot_pos = jnp.minimum(jnp.sum(earlier * onehot, axis=2), CAP)
    return (chosen.reshape(DOCS, DEC), slot_pos.reshape(DOCS, DEC))


def draw_expert_index(key, part):
    chosen, slot_pos = routing(key)
    return chosen


def draw_slot(key, part):
    chosen, slot_pos = routing(key)
    return slot_pos


def draw_router_logits(key, part):
    chosen, slot_pos = routing(key)
    key = jax.random.fold_in(key, 5)
    key_a = jax.random.fold_in(key, 0)
    marked = (chosen[:, :, None] == jnp.arange(EXPERTS, dtype=jnp.int32)[None, None, :]).astype(jnp.float32)
    noise = jnp.clip(jax.random.normal(key_a, (DOCS, DEC, EXPERTS)), -5.0, 5.0)
    logits = 1.5 * noise + 5.0 * marked
    return logits


def draw_resid(key, part):
    key = jax.random.fold_in(key, 11)
    key_a, key_b = jax.random.split(key)
    scale = jnp.exp(jax.random.uniform(key_b, (DOCS, DEC, 1), minval=0.0, maxval=2.302585))
    base = jnp.clip(jax.random.normal(key_a, (DOCS, DEC, D)), -6.0, 6.0)
    return (base * scale).astype(jnp.bfloat16)


def draw_queries(key, part):
    key = jax.random.fold_in(key, 7)
    base = jnp.clip(jax.random.normal(key, (DOCS, DEC, D)), -6.0, 6.0)
    return base.astype(jnp.bfloat16)


def draw_keys(key, part):
    key = jax.random.fold_in(key, 9)
    base = jnp.clip(jax.random.normal(key, (DOCS, ENC, D)), -6.0, 6.0)
    return base.astype(jnp.bfloat16)


def block_levels(stream_key, extent, shards, smallest, high):
    gain, own = 1.0, jax.random.fold_in(stream_key, 6)
    for dim, parts in shards:
        draws = jnp.exp(jax.random.uniform(jax.random.fold_in(own, dim), (parts,), jnp.float32, smallest / len(shards), high / len(shards)))
        gain = gain * jnp.repeat(draws, extent[dim] // parts).reshape([-1 if axis == dim else 1 for axis in range(len(extent))])
    return gain


def normal_values(rng, dims, spread, reach, pieces=(), held_as=jnp.bfloat16):
    drawn = spread * jax.random.normal(rng, dims, jnp.float32)
    if pieces:
        drawn = drawn * block_levels(rng, dims, pieces, -0.22, 0.18)
    return jnp.clip(drawn, -reach, reach).astype(held_as)


def setup_inputs(seed: int = 0) -> dict:
    seeds = jax.random.split(jax.random.key(seed), 13)
    resid = draw_resid(jax.random.fold_in(seeds[12], 71), 0)
    norm_gain = jnp.clip(1.0 + 0.18 * jax.random.normal(seeds[1], (D,), jnp.float32), 0.1, 1.9)
    router_logits = draw_router_logits(jax.random.fold_in(seeds[12], 71), 0)
    router_weight = normal_values(seeds[3], (D, EXPERTS), D ** -0.5, 0.125)
    expert_index = draw_expert_index(jax.random.fold_in(seeds[12], 71), 0)
    slot = draw_slot(jax.random.fold_in(seeds[12], 71), 0)
    w_in = normal_values(seeds[6], (EXPERTS, D, FF), D ** -0.5, 0.125, ((0, 32), (2, 16)))
    w_out = normal_values(seeds[7], (EXPERTS, FF, D), FF ** -0.5, 0.078125, ((0, 32), (1, 16)))
    grad_out = normal_values(seeds[8], (DOCS, DEC, D), 1.0, 6.0, ((0, 32), (1, 16)))
    queries = draw_queries(jax.random.fold_in(seeds[12], 71), 0)
    keys = draw_keys(jax.random.fold_in(seeds[12], 71), 0)
    values = normal_values(seeds[11], (DOCS, ENC, D), 1.0, 6.0, ((0, 32), (2, 16)))
    return {"resid": resid, "norm_gain": norm_gain, "router_logits": router_logits, "router_weight": router_weight, "expert_index": expert_index, "slot": slot, "w_in": w_in, "w_out": w_out, "grad_out": grad_out, "queries": queries, "keys": keys, "values": values}


EPSILON = 1e-06
SCORE_SCALE = 0.125
COEFF = 0.7978845608

def gelu_slope(hidden):
    tangent = jnp.tanh(COEFF * (hidden + 0.044715 * hidden * hidden * hidden))
    return 0.5 * (1.0 + tangent) + 0.5 * hidden * (1.0 - tangent * tangent) * COEFF * (1.0 + 0.134145 * hidden * hidden)

def gelu_value(hidden):
    tangent = jnp.tanh(COEFF * (hidden + 0.044715 * hidden * hidden * hidden))
    return 0.5 * hidden * (1.0 + tangent)

def reference(resid, norm_gain, router_logits, router_weight, expert_index, slot, w_in, w_out, grad_out, queries, keys, values):
    stream = resid.astype(jnp.float32)
    root_mean = jnp.sqrt(lax.optimization_barrier(jnp.mean(stream * stream, axis=-1, keepdims=True)) + EPSILON)
    normed = stream / root_mean
    normed_in = (normed * norm_gain).astype(jnp.bfloat16)
    router_probs = jax.nn.softmax(router_logits, axis=-1)
    kept_mask = slot < CAP
    onehot = (expert_index[..., None] == jnp.arange(EXPERTS, dtype=jnp.int32)).astype(jnp.float32)
    chosen = lax.optimization_barrier(jnp.sum(router_probs * onehot, axis=-1))
    upstream = grad_out.astype(jnp.float32)
    expert_ids = expert_index.reshape(DOCS, N_SEQ, TOK_DEV)
    slot_pos = slot.reshape(DOCS, N_SEQ, TOK_DEV)
    token_ids = jnp.arange(DOCS * DEC, dtype=jnp.int32).reshape(DOCS, N_SEQ, TOK_DEV)
    seq_ids = jnp.broadcast_to(jnp.arange(N_SEQ, dtype=jnp.int32)[None, :, None], expert_ids.shape)
    doc_ids = jnp.broadcast_to(jnp.arange(DOCS, dtype=jnp.int32)[:, None, None], expert_ids.shape)
    slot_table = jnp.full((EXPERTS, N_SEQ, DOCS, CAP + 1), -1, jnp.int32)
    slot_table = slot_table.at[expert_ids, seq_ids, doc_ids, slot_pos].set(token_ids)
    flat_in = normed_in.reshape(DOCS * DEC, D)
    flat_grad = grad_out.reshape(DOCS * DEC, D)

    def expert_term(expert):
        ids = slot_table[expert, :, :, :CAP].reshape(-1)
        valid = (ids >= 0)[:, None]
        safe = jnp.maximum(ids, 0)
        slot_inputs = jnp.where(valid, flat_in[safe], jnp.zeros((), jnp.bfloat16))
        slot_grads = jnp.where(valid, flat_grad[safe], jnp.zeros((), jnp.bfloat16))
        weight_in = w_in[expert]
        hidden = jnp.dot(slot_inputs, weight_in, preferred_element_type=jnp.float32)
        hidden_grad = lax.dot_general(slot_grads, w_out[expert], (((1,), (1,)), ((), ())), preferred_element_type=jnp.float32)
        scaled_grad = (hidden_grad * gelu_slope(hidden)).astype(jnp.bfloat16)
        products = gelu_value(hidden) * hidden_grad
        gate_parts = lax.optimization_barrier(jnp.sum(products.reshape(-1, N_SEQ, HID), axis=2))
        gate_parts = lax.optimization_barrier(gate_parts.astype(jnp.bfloat16))
        gate_dot = lax.optimization_barrier(jnp.sum(gate_parts.astype(jnp.float32), axis=1))
        partials = jnp.einsum('skh,dkh->skd', scaled_grad.reshape(-1, N_SEQ, HID).astype(jnp.float32), weight_in.reshape(D, N_SEQ, HID).astype(jnp.float32))
        rounded = lax.optimization_barrier(partials.astype(jnp.bfloat16))
        return (lax.optimization_barrier(jnp.sum(rounded.astype(jnp.float32), axis=1)), gate_dot)
    results, gates = lax.map(expert_term, jnp.arange(EXPERTS, dtype=jnp.int32))
    results = results.reshape(EXPERTS, N_SEQ, DOCS, CAP, D)
    gates = gates.reshape(EXPERTS, N_SEQ, DOCS, CAP)
    last_slot = jnp.minimum(slot_pos, CAP - 1)
    fetched = results[expert_ids, seq_ids, doc_ids, last_slot].reshape(DOCS, DEC, D)
    fetched_gate = gates[expert_ids, seq_ids, doc_ids, last_slot].reshape(DOCS, DEC)
    dispatch_grad = jnp.where(kept_mask[..., None], chosen[..., None] * fetched, 0.0)
    prob_grad = jnp.where(kept_mask, fetched_gate, 0.0)
    logit_grad = prob_grad[..., None] * chosen[..., None] * (onehot - router_probs)
    router_term = jnp.dot(logit_grad.reshape(-1, EXPERTS), router_weight.astype(jnp.float32).T, precision=lax.Precision.HIGHEST).reshape(DOCS, DEC, D)
    normed_grad = (dispatch_grad + router_term) * norm_gain
    stream_grad = upstream + (normed_grad - normed * lax.optimization_barrier(jnp.mean(normed_grad * normed, axis=-1, keepdims=True))) / root_mean
    grad_stream = stream_grad.astype(jnp.bfloat16)

    def attend(items):
        query_doc, key_doc, value_doc, context_doc = items
        query_heads = query_doc.reshape(DEC, HEADS, HEAD_DIM).astype(jnp.float32)
        key_heads = key_doc.reshape(ENC, HEADS, HEAD_DIM).astype(jnp.float32)
        value_heads = value_doc.reshape(ENC, HEADS, HEAD_DIM).astype(jnp.float32)
        context_heads = context_doc.reshape(DEC, HEADS, HEAD_DIM).astype(jnp.float32)
        scores = jnp.einsum('qhd,khd->hqk', query_heads, key_heads) * SCORE_SCALE
        att_probs = jax.nn.softmax(scores, axis=-1)
        prob_grads = jnp.einsum('qhd,khd->hqk', context_heads, value_heads)
        delta = lax.optimization_barrier(jnp.sum(att_probs * prob_grads, axis=-1, keepdims=True))
        score_grads = att_probs * (prob_grads - delta)
        att_weights = att_probs.astype(jnp.bfloat16).astype(jnp.float32)
        score_weights = score_grads.astype(jnp.bfloat16).astype(jnp.float32)
        blocked_scores = score_weights.reshape(HEADS, N_SEQ, TOK_DEV, ENC)
        blocked_weights = att_weights.reshape(HEADS, N_SEQ, TOK_DEV, ENC)
        key_parts = jnp.einsum('hsqk,sqhd->skhd', blocked_scores, query_heads.reshape(N_SEQ, TOK_DEV, HEADS, HEAD_DIM)) * SCORE_SCALE
        value_parts = jnp.einsum('hsqk,sqhd->skhd', blocked_weights, context_heads.reshape(N_SEQ, TOK_DEV, HEADS, HEAD_DIM))
        key_parts = lax.optimization_barrier(key_parts.astype(jnp.bfloat16))
        value_parts = lax.optimization_barrier(value_parts.astype(jnp.bfloat16))
        key_grad = lax.optimization_barrier(jnp.sum(key_parts.astype(jnp.float32), axis=0)).astype(jnp.bfloat16)
        value_grad = lax.optimization_barrier(jnp.sum(value_parts.astype(jnp.float32), axis=0)).astype(jnp.bfloat16)
        return (key_grad.reshape(ENC, D), value_grad.reshape(ENC, D))
    grad_keys, grad_values = lax.map(attend, (queries, keys, values, grad_stream))
    return (grad_stream, grad_keys, grad_values)
```

```python
import functools

import jax
import jax.numpy as jnp
from jax import lax
from jax.experimental import pallas as pl
from jax.experimental.pallas import tpu as pltpu
from jax.sharding import PartitionSpec as P

D = 2048
EXPERTS = 32
CAP = 3
SLOTS = EXPERTS * CAP
ENC = 64
TOK = 128
N_Y = 2
N_Z = 8
HID = 320
EPSILON = 1e-06
SCORE_SCALE = 0.125
COEFF = 0.7978845608
BF16 = jnp.bfloat16
F32 = jnp.float32
WIDE = D + 128
VMEM = 40 * 1024 * 1024


def dot(a, b, dims=((1,), (0,)), **kw):
    return lax.dot_general(a, b, (dims, ((), ())), preferred_element_type=F32, **kw)


def shuffle_matrix():
    row = lax.broadcasted_iota(jnp.int32, (512, 512), 0)
    col = lax.broadcasted_iota(jnp.int32, (512, 512), 1)
    return ((row // 16 == col % 32) & (row % 16 == col // 32)).astype(F32).astype(BF16)


def slot_table(ids, slot):
    target = jnp.where(slot < CAP, slot * EXPERTS + ids, -1)
    rows = lax.broadcasted_iota(jnp.int32, (SLOTS, TOK), 0)
    return (rows == target).astype(F32).astype(BF16)


def whole(shape):
    return pl.BlockSpec(shape, lambda i: (0,) * len(shape))


def call(kernel, ins, outs, in_specs=None, scratch=(), flops=0, name=None):
    in_specs = in_specs or [None] * len(ins)
    specs = [s or whole(a.shape) for s, a in zip(in_specs, ins)]
    moved = sum(a.size * a.dtype.itemsize for a in ins)
    moved += sum(o.size * o.dtype.itemsize for o in outs)
    return pl.pallas_call(
        kernel,
        grid=(1,),
        in_specs=specs,
        out_specs=[whole(o.shape) for o in outs],
        out_shape=outs,
        scratch_shapes=list(scratch),
        compiler_params=pltpu.CompilerParams(vmem_limit_bytes=VMEM),
        cost_estimate=pl.CostEstimate(flops=flops, bytes_accessed=moved, transcendentals=0),
        name=name,
    )(*ins)


def shape(dims, dtype=BF16):
    return jax.ShapeDtypeStruct(dims, dtype)


def dispatch_kernel(resid_ref, grad_ref, gain_ref, ids_ref, slot_ref, out_ref, rows_ref):
    stream = resid_ref[...].astype(F32)
    root_mean = jnp.sqrt(jnp.mean(stream * stream, axis=-1, keepdims=True) + EPSILON)
    normed_in = (stream / root_mean * gain_ref[...]).astype(BF16)
    table = slot_table(ids_ref[...], slot_ref[...])
    for half, source in enumerate((normed_in, grad_ref[...])):
        picked = dot(table, source).astype(BF16)
        for part in range(8):
            for c in range(CAP):
                row = (half * 8 + part) * 32
                rows_ref[row : row + 32, c * 256 : (c + 1) * 256] = picked[
                    c * 32 : (c + 1) * 32, part * 256 : (part + 1) * 256
                ]
    out_ref[...] = dot(shuffle_matrix(), rows_ref[...]).astype(BF16)


def collect_kernel(in_ref, kv_ref, kv_other_ref, out_ref):
    rows = dot(shuffle_matrix(), in_ref[...], ((0,), (0,))).astype(BF16)
    for half in range(2):
        for part in range(8):
            for c in range(CAP):
                row = (half * 8 + part) * 32
                out_ref[
                    half * 96 + c * 32 : half * 96 + (c + 1) * 32, part * 256 : (part + 1) * 256
                ] = rows[row : row + 32, c * 256 : (c + 1) * 256]
    for i in range(8):
        out_ref[192:208, i * 128 : (i + 1) * 128] = kv_ref[i * 16 : (i + 1) * 16, :]
        out_ref[192:208, (i + 8) * 128 : (i + 9) * 128] = kv_other_ref[i * 16 : (i + 1) * 16, :]


def expert_kernel(n, split, *refs):
    in_refs, grad_refs = refs[:n], refs[n : 2 * n]
    w_in_refs, w_out_refs = refs[2 * n : 2 * n + 2], refs[2 * n + 2 : 2 * n + 4]
    out_refs = refs[2 * n + 4 :]
    inputs = jnp.concatenate([r[...] for r in in_refs], axis=0) if n > 1 else in_refs[0][...]
    grads = jnp.concatenate([r[...] for r in grad_refs], axis=0) if n > 1 else grad_refs[0][...]
    total, gate = None, None
    for w_in_ref, w_out_ref in zip(w_in_refs, w_out_refs):
        hidden = dot(inputs, w_in_ref[...])
        hidden_grad = dot(grads, w_out_ref[...], ((1,), (1,)))
        square = hidden * hidden
        tangent = jnp.tanh(COEFF * (hidden + 0.044715 * square * hidden))
        half = 0.5 * (1.0 + tangent)
        slope = half + 0.5 * hidden * (1.0 - tangent * tangent) * COEFF * (1.0 + 0.134145 * square)
        scaled = (hidden_grad * slope).astype(BF16)
        part = dot(scaled, w_in_ref[...], ((1,), (1,)))
        gates = jnp.sum(half * hidden * hidden_grad, axis=1, keepdims=True)
        total = part if total is None else total + part
        gate = gates if gate is None else gate + gates
    total = total.astype(BF16)
    gate = jnp.broadcast_to(gate, (n * 96, 128)).astype(BF16)
    size = 48 if split else 96
    for i, out_ref in enumerate(out_refs):
        out_ref[:, :D] = total[i * size : (i + 1) * size]
        out_ref[:, D:] = gate[i * size : (i + 1) * size]


def experts(blocks, weights, split=False, name=None):
    n = len(blocks)
    ins = [b[0] for b in blocks] + [b[1] for b in blocks] + list(weights)
    specs = [pl.BlockSpec((96, D), lambda i, k=b[2]: (k, 0)) for b in blocks]
    specs += [pl.BlockSpec((96, D), lambda i, k=b[3]: (k, 0)) for b in blocks]
    specs += [None] * 4
    outs = [shape((48, WIDE))] * 2 if split else [shape((96, WIDE))] * n
    return call(
        functools.partial(expert_kernel, n, split),
        ins,
        outs,
        specs,
        flops=2 * n * 96 * D * 2 * HID * 3,
        name=name,
    )


def return_kernel(own_ref, up_ref, down_ref, out_ref, rows_ref):
    total = own_ref[...].astype(F32) + up_ref[...].astype(F32) + down_ref[...].astype(F32)
    total = total.astype(BF16)
    rows_ref[:, 384:] = jnp.zeros((512, 128), BF16)
    for c in range(CAP):
        for part in range(16):
            rows_ref[part * 32 : (part + 1) * 32, c * 128 : (c + 1) * 128] = total[
                c * 32 : (c + 1) * 32, part * 128 : (part + 1) * 128
            ]
        rows_ref[c * 32 : (c + 1) * 32, 384:] = total[c * 32 : (c + 1) * 32, D:]
    out_ref[...] = dot(shuffle_matrix(), rows_ref[...]).astype(BF16)


def stream_kernel(
    in_ref, resid_ref, grad_ref, gain_ref, logits_ref, weight_ref, ids_ref, slot_ref, out_ref,
    rows_ref,
):
    rows = dot(shuffle_matrix(), in_ref[...], ((0,), (0,))).astype(BF16)
    for c in range(CAP):
        for part in range(16):
            rows_ref[c * 32 : (c + 1) * 32, part * 128 : (part + 1) * 128] = rows[
                part * 32 : (part + 1) * 32, c * 128 : (c + 1) * 128
            ]
        rows_ref[c * 32 : (c + 1) * 32, D:] = rows[c * 32 : (c + 1) * 32, 384:]
    ids = ids_ref[...]
    fetched = dot(slot_table(ids, slot_ref[...]), rows_ref[...], ((0,), (0,)))
    prob_grad = fetched[:, D : D + 1]
    logits = logits_ref[...]
    powers = jnp.exp(logits - jnp.max(logits, axis=-1, keepdims=True))
    probs = powers / jnp.sum(powers, axis=-1, keepdims=True)
    by_expert = lax.broadcasted_iota(jnp.int32, (EXPERTS, TOK), 0) == ids
    eye = lax.broadcasted_iota(jnp.int32, (EXPERTS, EXPERTS), 0) == lax.broadcasted_iota(
        jnp.int32, (EXPERTS, EXPERTS), 1
    )
    onehot = dot(by_expert.astype(F32).astype(BF16), eye.astype(F32).astype(BF16), ((0,), (0,)))
    chosen = jnp.sum(probs * onehot, axis=-1, keepdims=True)
    logit_grad = prob_grad * chosen * (onehot - probs)
    router_term = dot(
        logit_grad, weight_ref[...].astype(F32), ((1,), (1,)), precision=lax.Precision.HIGHEST
    )
    stream = resid_ref[...].astype(F32)
    root_mean = jnp.sqrt(jnp.mean(stream * stream, axis=-1, keepdims=True) + EPSILON)
    normed = stream / root_mean
    normed_grad = (chosen * fetched[:, :D] + router_term) * gain_ref[...]
    mean = jnp.mean(normed_grad * normed, axis=-1, keepdims=True)
    out_ref[...] = (
        grad_ref[...].astype(F32) + (normed_grad - normed * mean) / root_mean
    ).astype(BF16)


def head_mask():
    row = lax.broadcasted_iota(jnp.int32, (256, 256), 0)
    col = lax.broadcasted_iota(jnp.int32, (256, 256), 1)
    return row // ENC == col // ENC


def by_head(rows, mask):
    return jnp.where(mask, jnp.concatenate([rows.astype(F32)] * 4, axis=0), 0.0).astype(BF16)


def probs_kernel(place_ref, *refs):
    block_refs, query_ref, probs_ref, values_ref, keys_ref = (
        refs[:8], refs[8], refs[9], refs[10], refs[11],
    )
    for i, block_ref in enumerate(block_refs):
        for other in range(2):
            lanes = pl.ds(pl.multiple_of(place_ref[2 * i + other] * 128, 128), 128)
            for k in range(4):
                base = (other * 8 + k) * 128
                keys_ref[k * 16 : (k + 1) * 16, lanes] = block_ref[:, base : base + 128]
                values_ref[k * 16 : (k + 1) * 16, lanes] = block_ref[:, base + 512 : base + 640]
    mask = head_mask()
    for g in range(8):
        cols = slice(g * 256, (g + 1) * 256)
        scores = dot(by_head(keys_ref[:, cols], mask), query_ref[:, cols], ((1,), (1,)))
        scores = (scores * SCORE_SCALE).reshape(4, ENC, TOK)
        powers = jnp.exp(scores - jnp.max(scores, axis=1, keepdims=True))
        probs = powers / jnp.sum(powers, axis=1, keepdims=True)
        probs_ref[g] = probs.reshape(256, TOK)


def attend_kernel(probs_ref, values_ref, query_ref, stream_ref, out_ref):
    mask = head_mask()
    for g in range(8):
        cols = slice(g * 256, (g + 1) * 256)
        probs = probs_ref[g]
        context, query = stream_ref[:, cols], query_ref[:, cols]
        prob_grads = dot(by_head(values_ref[:, cols], mask), context, ((1,), (1,)))
        delta = jnp.sum((probs * prob_grads).reshape(4, ENC, TOK), axis=1, keepdims=True)
        delta = jnp.broadcast_to(delta, (4, ENC, TOK)).reshape(256, TOK)
        score_weights = (probs * (prob_grads - delta)).astype(BF16)
        key_terms = jnp.where(mask, dot(score_weights, query), 0.0)
        value_terms = jnp.where(mask, dot(probs.astype(BF16), context), 0.0)
        key_terms = jnp.sum(key_terms.reshape(4, ENC, 256), axis=0) * SCORE_SCALE
        value_terms = jnp.sum(value_terms.reshape(4, ENC, 256), axis=0)
        for half in range(2):
            row = (2 * g + half) * 128
            lanes = slice(half * 128, (half + 1) * 128)
            out_ref[row : row + 64] = key_terms[:, lanes].astype(BF16)
            out_ref[row + 64 : row + 128] = value_terms[:, lanes].astype(BF16)


def seq_pairs(step):
    return [
        (y * N_Z + z, ((y + step[0]) % N_Y) * N_Z + (z + step[1]) % N_Z)
        for y in range(N_Y)
        for z in range(N_Z)
    ]


def shift(a, step):
    return lax.ppermute(a, "seq", seq_pairs(step))


UP, DOWN, ACROSS = (0, 1), (0, -1), (1, 0)


def plus(a, b):
    return (a.astype(F32) + b.astype(F32)).astype(BF16)


def body(
    resid,
    norm_gain,
    router_logits,
    router_weight,
    expert_index,
    slot,
    w_in,
    w_out,
    grad_out,
    queries,
    keys,
    values,
):
    seq = lax.axis_index("seq")
    gain = norm_gain.reshape(1, D)
    stream, upstream, query = resid[0], grad_out[0], queries[0]
    kv = jnp.concatenate([keys[0], values[0]], axis=0)
    kv_other = shift(kv, ACROSS)
    (outgoing,) = call(
        dispatch_kernel,
        [stream, upstream, gain, expert_index, slot],
        [shape((512, 768))],
        scratch=[pltpu.VMEM((512, 768), BF16)],
        flops=2 * 512 * 512 * 768,
        name="dispatch",
    )
    arrived = lax.all_to_all(outgoing, "exp", 0, 0, tiled=True)
    (block,) = call(
        collect_kernel,
        [arrived, kv, kv_other],
        [shape((208, D))],
        flops=2 * 512 * 512 * 768,
        name="collect",
    )
    block, own_in, own_out = lax.optimization_barrier((block, w_in[0], w_out[0]))
    ups, downs = [block], [block]
    for _ in range(3):
        ups.append(shift(ups[-1], UP))
        downs.append(shift(downs[-1], DOWN))
    far_in = shift(ups[3][:96], UP)
    far_grad = shift(downs[3][96:], DOWN)
    weights = (own_in, shift(own_in, ACROSS), own_out, shift(own_out, ACROSS))

    (own,) = experts([(block, block, 0, 1)], weights, name="experts_0")
    up_parts, down_parts = [own], [own]
    for k in (1, 2, 3):
        a, b = experts(
            [(ups[k], ups[k], 0, 1), (downs[k], downs[k], 0, 1)], weights, name=f"experts_{k}"
        )
        up_parts.append(a)
        down_parts.append(b)
    far_a, far_b = experts([(far_in, far_grad, 0, 0)], weights, split=True, name="experts_4")

    back, forth = shift(far_a, DOWN), shift(far_b, UP)
    back = jnp.concatenate([plus(up_parts[3][:48], back), up_parts[3][48:]], axis=0)
    forth = jnp.concatenate([down_parts[3][:48], plus(down_parts[3][48:], forth)], axis=0)
    for k in (2, 1):
        back = plus(shift(back, DOWN), up_parts[k])
        forth = plus(shift(forth, UP), down_parts[k])
    back, forth = shift(back, DOWN), shift(forth, UP)

    z, y = seq % N_Z, seq // N_Z
    places = []
    for step in (0, -1, 1, -2, 2, -3, 3, 4):
        at = (z + step + N_Z) % N_Z
        places += [y * N_Z + at, (1 - y) * N_Z + at]
    kv_blocks = [block, ups[1], downs[1], ups[2], downs[2], ups[3], downs[3], far_grad]
    probs, all_values = call(
        probs_kernel,
        [jnp.stack(places).astype(jnp.int32)] + kv_blocks + [query],
        [shape((8, 256, TOK), F32), shape((ENC, D))],
        [pl.BlockSpec(memory_space=pltpu.SMEM)]
        + [pl.BlockSpec((16, D), lambda i, k=k: (k, 0)) for k in [12] * 7 + [6]]
        + [None],
        scratch=[pltpu.VMEM((ENC, D), BF16)],
        flops=8 * 2 * 256 * 256 * 128,
        name="probs",
    )

    (returning,) = call(
        return_kernel,
        [own, back, forth],
        [shape((512, 512))],
        scratch=[pltpu.VMEM((512, 512), BF16)],
        flops=2 * 512 * 512 * 512,
        name="return",
    )
    returned = lax.all_to_all(returning, "exp", 0, 0, tiled=True)
    (grad_stream,) = call(
        stream_kernel,
        [
            returned, stream, upstream, gain, router_logits[0], router_weight, expert_index, slot,
        ],
        [shape((TOK, D))],
        scratch=[pltpu.VMEM((SLOTS, WIDE), BF16)],
        flops=2 * 512 * 512 * 512,
        name="stream",
    )
    (terms,) = call(
        attend_kernel,
        [probs, all_values, query, grad_stream],
        [shape((2048, 128))],
        flops=8 * 3 * 2 * 256 * 256 * 128,
        name="attend",
    )
    terms = lax.all_to_all(terms, "seq", 0, 0, tiled=True)
    totals = jnp.sum(terms.reshape(16, 2, ENC, 128).astype(F32), axis=0).astype(BF16)
    return (grad_stream[None], totals[0][None], totals[1][None])


def solution(mesh):
    in_specs = (
        P("exp", "seq", None),
        P(),
        P("exp", "seq", None),
        P(),
        P("exp", "seq"),
        P("exp", "seq"),
        P("exp", None, "seq"),
        P("exp", "seq", None),
        P("exp", "seq", None),
        P("exp", "seq", None),
        P("exp", None, "seq"),
        P("exp", None, "seq"),
    )
    out_specs = (P("exp", "seq", None), P("exp", None, "seq"), P("exp", None, "seq"))
    return jax.shard_map(body, mesh=mesh, in_specs=in_specs, out_specs=out_specs, check_vma=False)
```

```python
import functools

import jax
import jax.numpy as jnp
from jax import lax
from jax.experimental import pallas as pl
from jax.experimental.pallas import tpu as pltpu
from jax.sharding import PartitionSpec as P

D = 2048
EXPERTS = 32
CAP = 3
SLOTS = EXPERTS * CAP
ENC = 64
TOK = 128
N_Y = 2
N_Z = 8
HID = 320
EPSILON = 1e-06
SCORE_SCALE = 0.125
COEFF = 0.7978845608
BF16 = jnp.bfloat16
F32 = jnp.float32
WIDE = D + 128


def dot(a, b, dims=((1,), (0,)), **kw):
    return lax.dot_general(a, b, (dims, ((), ())), preferred_element_type=F32, **kw)


def shuffle_matrix():
    row = lax.broadcasted_iota(jnp.int32, (512, 512), 0)
    col = lax.broadcasted_iota(jnp.int32, (512, 512), 1)
    return ((row // 16 == col % 32) & (row % 16 == col // 32)).astype(F32).astype(BF16)


def slot_table(target):
    rows = lax.broadcasted_iota(jnp.int32, (SLOTS, TOK), 0).astype(F32)
    return (rows == target).astype(F32).astype(BF16)


def call(kernel, ins, outs, hbm=(), scratch=(), flops=0, limit=16, name=None):
    specs = [
        pl.BlockSpec(memory_space=pltpu.MemorySpace.HBM if i in hbm else pltpu.MemorySpace.VMEM)
        for i in range(len(ins))
    ]
    n = len(ins) + len(outs) + len(scratch)

    def run(*refs):
        given, held, sems = list(refs[:n]), refs[n:-1], refs[-1]
        for k, i in enumerate(hbm):
            copy = pltpu.make_async_copy(given[i], held[k], sems.at[k])
            copy.start()
            given[i] = functools.partial(arrived, copy, held[k])
        kernel(*given)

    return pl.pallas_call(
        run if hbm else kernel,
        in_specs=specs,
        out_specs=[pl.BlockSpec(memory_space=pltpu.MemorySpace.VMEM)] * len(outs),
        out_shape=outs,
        scratch_shapes=list(scratch)
        + [pltpu.VMEM(ins[i].shape, ins[i].dtype) for i in hbm]
        + ([pltpu.SemaphoreType.DMA((len(hbm),))] if hbm else []),
        compiler_params=pltpu.CompilerParams(vmem_limit_bytes=limit * 1024 * 1024),
        cost_estimate=pl.CostEstimate(flops=flops, bytes_accessed=0, transcendentals=0),
        name=name,
    )(*ins)


def arrived(copy, ref):
    copy.wait()
    return ref


def shape(dims, dtype=BF16):
    return jax.ShapeDtypeStruct(dims, dtype)


def dispatch_kernel(
    resid_ref, grad_ref, gain_ref, ids_ref, slot_ref, logits_ref, out_ref, token_ref, rows_ref
):
    stream = resid_ref()[...].astype(F32)
    root_mean = jnp.sqrt(jnp.mean(stream * stream, axis=-1, keepdims=True) + EPSILON)
    normed_in = (stream / root_mean * gain_ref()[...]).astype(BF16)
    ids, slot = ids_ref()[...], slot_ref()[...]
    target = jnp.where(slot < CAP, slot * EXPERTS + ids, -1).astype(F32)
    logits = logits_ref()[...]
    powers = jnp.exp(logits - jnp.max(logits, axis=0, keepdims=True))
    probs = powers / jnp.sum(powers, axis=0, keepdims=True)
    onehot = (lax.broadcasted_iota(jnp.int32, (EXPERTS, TOK), 0) == ids).astype(F32)
    chosen = jnp.sum(probs * onehot, axis=0, keepdims=True)
    token_ref[:EXPERTS] = chosen * (onehot - probs)
    token_ref[EXPERTS : EXPERTS + 8] = jnp.concatenate([chosen] * 4 + [target] * 4, axis=0)
    table = slot_table(target)
    for half, source in enumerate((normed_in, grad_ref()[...])):
        picked = dot(table, source).astype(BF16)
        for part in range(8):
            for c in range(CAP):
                row = (half * 8 + part) * 32
                rows_ref[row : row + 32, c * 256 : (c + 1) * 256] = picked[
                    c * 32 : (c + 1) * 32, part * 256 : (part + 1) * 256
                ]
    out_ref[...] = dot(shuffle_matrix(), rows_ref[...]).astype(BF16)


def collect_kernel(in_ref, kv_ref, kv_other_ref, out_ref):
    rows = dot(shuffle_matrix(), in_ref[...], ((0,), (0,))).astype(BF16)
    for half in range(2):
        for part in range(8):
            for c in range(CAP):
                row = (half * 8 + part) * 32
                out_ref[
                    half * 96 + c * 32 : half * 96 + (c + 1) * 32, part * 256 : (part + 1) * 256
                ] = rows[row : row + 32, c * 256 : (c + 1) * 256]
    for i in range(8):
        out_ref[192:208, i * 128 : (i + 1) * 128] = kv_ref[i * 16 : (i + 1) * 16, :]
        out_ref[192:208, (i + 8) * 128 : (i + 9) * 128] = kv_other_ref[i * 16 : (i + 1) * 16, :]


def expert_kernel(n, split, *refs):
    pairs, weight_refs = refs[: 2 * n], refs[2 * n : 2 * n + 4]
    out_refs, kv_ref = refs[2 * n + 4 : -1], refs[-1]
    for i, ref in enumerate(pairs[n:]):
        kv_ref[i * 16 : (i + 1) * 16] = ref[ref.shape[0] - 16 :]
    if split:
        inputs, grads = pairs[0][:96], pairs[1][:96]
    else:
        inputs = jnp.concatenate([r[:96] for r in pairs[:n]], axis=0)
        grads = jnp.concatenate([r[96:192] for r in pairs[:n]], axis=0)
    total, gate = None, None
    for k in range(2):
        w_in, w_out = weight_refs[2 * k]()[...], weight_refs[2 * k + 1]()[...]
        hidden = dot(inputs, w_in, ((1,), (1,)))
        hidden_grad = dot(grads, w_out, ((1,), (1,)))
        square = hidden * hidden
        tangent = jnp.tanh(COEFF * (hidden + 0.044715 * square * hidden))
        half = 0.5 * (1.0 + tangent)
        slope = half + 0.5 * hidden * (1.0 - tangent * tangent) * COEFF * (1.0 + 0.134145 * square)
        scaled = (hidden_grad * slope).astype(BF16)
        part = dot(scaled, w_in)
        gates = jnp.sum(half * hidden * hidden_grad, axis=1, keepdims=True)
        total = part if total is None else total + part
        gate = gates if gate is None else gate + gates
    total = total.astype(BF16)
    gate = jnp.broadcast_to(gate, (gate.shape[0], 128)).astype(BF16)
    size = 48 if split else 96
    for i, out_ref in enumerate(out_refs):
        out_ref[:, :D] = total[i * size : (i + 1) * size]
        out_ref[:, D:] = gate[i * size : (i + 1) * size]


def experts(blocks, weights, split=False, name=None):
    n = 1 if split else len(blocks)
    outs = [shape((48, WIDE))] * 2 if split else [shape((96, WIDE))] * n
    outs.append(shape((16 * n, D)))
    kernel = functools.partial(expert_kernel, n, split)
    if not split:
        kernel = lambda *refs: expert_kernel(n, False, *refs[:n], *refs[:n], *refs[n:])
    return call(
        kernel,
        list(blocks) + list(weights),
        outs,
        hbm=tuple(range(len(blocks), len(blocks) + 4)),
        flops=2 * n * 96 * D * 2 * HID * 3,
        limit=12 if split else 40,
        name=name,
    )


def return_kernel(*refs):
    parts, out_ref, rows_ref = refs[:5], refs[5], refs[6]
    total = parts[0][...].astype(F32)
    for ref in parts[1:]:
        total = total + ref[...].astype(F32)
    total = total.astype(BF16)
    rows_ref[:, 384:] = jnp.zeros((512, 128), BF16)
    for c in range(CAP):
        for part in range(16):
            rows_ref[part * 32 : (part + 1) * 32, c * 128 : (c + 1) * 128] = total[
                c * 32 : (c + 1) * 32, part * 128 : (part + 1) * 128
            ]
        rows_ref[c * 32 : (c + 1) * 32, 384:] = total[c * 32 : (c + 1) * 32, D:]
    out_ref[...] = dot(shuffle_matrix(), rows_ref[...]).astype(BF16)


def stream_kernel(
    in_ref, token_ref, probs_ref, values_ref, weight_ref, resid_ref, gain_ref, grad_ref, query_ref,
    out_ref, terms_ref, rows_ref,
):
    rows = dot(shuffle_matrix(), in_ref[...], ((0,), (0,))).astype(BF16)
    for c in range(CAP):
        for part in range(16):
            rows_ref[c * 32 : (c + 1) * 32, part * 128 : (part + 1) * 128] = rows[
                part * 32 : (part + 1) * 32, c * 128 : (c + 1) * 128
            ]
        rows_ref[c * 32 : (c + 1) * 32, D:] = rows[c * 32 : (c + 1) * 32, 384:]
    chosen, target = token_ref[EXPERTS : EXPERTS + 1], token_ref[EXPERTS + 4 : EXPERTS + 5]
    table = slot_table(target)
    fetched = dot(table, rows_ref[:, :D], ((0,), (0,)))
    prob_grad = dot(rows_ref[:, D:], table, ((0,), (0,)))[:1]
    logit_grad = prob_grad * token_ref[:EXPERTS]
    router_term = dot(
        logit_grad, weight_ref()[...].astype(F32), ((0,), (0,)), precision=lax.Precision.HIGHEST
    )
    chosen = jnp.transpose(jnp.broadcast_to(chosen, (TOK, TOK)))[:, :1]
    stream = resid_ref()[...].astype(F32)
    root_mean = jnp.sqrt(jnp.mean(stream * stream, axis=-1, keepdims=True) + EPSILON)
    normed = stream / root_mean
    normed_grad = (chosen * fetched + router_term) * gain_ref()[...]
    mean = jnp.mean(normed_grad * normed, axis=-1, keepdims=True)
    out_ref[...] = (
        grad_ref()[...].astype(F32) + (normed_grad - normed * mean) / root_mean
    ).astype(BF16)
    attend(probs_ref(), values_ref(), query_ref(), out_ref, terms_ref)


def head_mask():
    row = lax.broadcasted_iota(jnp.int32, (256, 256), 0)
    col = lax.broadcasted_iota(jnp.int32, (256, 256), 1)
    return row // ENC == col // ENC


def by_head(rows, mask):
    return jnp.where(mask, jnp.concatenate([rows.astype(F32)] * 4, axis=0), 0.0).astype(BF16)


def probs_kernel(place_ref, query_ref, *refs):
    block_refs, probs_ref, values_ref, keys_ref = refs[:2], refs[2], refs[3], refs[4]
    blocks = [(r, k * 16) for r in block_refs for k in range(r.shape[0] // 16)]
    for i, (block_ref, first) in enumerate(blocks):
        for other in range(2):
            lanes = pl.ds(pl.multiple_of(place_ref[2 * i + other] * 128, 128), 128)
            for k in range(4):
                base = (other * 8 + k) * 128
                keys_ref[k * 16 : (k + 1) * 16, lanes] = block_ref[
                    first : first + 16, base : base + 128
                ]
                values_ref[k * 16 : (k + 1) * 16, lanes] = block_ref[
                    first : first + 16, base + 512 : base + 640
                ]
    mask = head_mask()
    query_ref = query_ref()
    for g in range(8):
        cols = slice(g * 256, (g + 1) * 256)
        scores = dot(by_head(keys_ref[:, cols], mask), query_ref[:, cols], ((1,), (1,)))
        scores = (scores * SCORE_SCALE).reshape(4, ENC, TOK)
        powers = jnp.exp(scores - jnp.max(scores, axis=1, keepdims=True))
        probs = powers / jnp.sum(powers, axis=1, keepdims=True)
        probs_ref[g] = probs.reshape(256, TOK)


def attend(probs_ref, values_ref, query_ref, stream_ref, out_ref):
    mask = head_mask()
    for g in range(8):
        cols = slice(g * 256, (g + 1) * 256)
        probs = probs_ref[g]
        context, query = stream_ref[:, cols], query_ref[:, cols]
        prob_grads = dot(by_head(values_ref[:, cols], mask), context, ((1,), (1,)))
        delta = jnp.sum((probs * prob_grads).reshape(4, ENC, TOK), axis=1, keepdims=True)
        delta = jnp.broadcast_to(delta, (4, ENC, TOK)).reshape(256, TOK)
        score_weights = (probs * (prob_grads - delta)).astype(BF16)
        key_terms = jnp.where(mask, dot(score_weights, query), 0.0)
        value_terms = jnp.where(mask, dot(probs.astype(BF16), context), 0.0)
        key_terms = jnp.sum(key_terms.reshape(4, ENC, 256), axis=0) * SCORE_SCALE
        value_terms = jnp.sum(value_terms.reshape(4, ENC, 256), axis=0)
        for half in range(2):
            row = (2 * g + half) * 128
            lanes = slice(half * 128, (half + 1) * 128)
            out_ref[row : row + 64] = key_terms[:, lanes].astype(BF16)
            out_ref[row + 64 : row + 128] = value_terms[:, lanes].astype(BF16)


def shift(a, step):
    pairs = []
    for y in range(N_Y):
        for z in range(N_Z):
            for e in range(EXPERTS):
                to = (z + (step if e % 2 == 0 else -step)) % N_Z
                pairs.append(((y * N_Z + z) * EXPERTS + e, (y * N_Z + to) * EXPERTS + e))
    return lax.ppermute(a, ("seq", "exp"), pairs)


def across(a):
    return lax.ppermute(a, "seq", [(s, (s + N_Z) % (N_Y * N_Z)) for s in range(N_Y * N_Z)])


FIRST, LAST = ((0, 48), (0, 0)), ((48, 0), (0, 0))


def plus(*parts):
    return functools.reduce(jnp.add, [a.astype(F32) for a in parts]).astype(BF16)


def call_probs(places, query, blocks):
    def run(place_ref, query_ref, *refs):
        held, sem = refs[-2:]
        copy = pltpu.make_async_copy(query_ref, held, sem)
        copy.start()
        probs_kernel(place_ref, functools.partial(arrived, copy, held), *refs[:-2])

    vmem = pl.BlockSpec(memory_space=pltpu.MemorySpace.VMEM)
    return pl.pallas_call(
        run,
        in_specs=[
            pl.BlockSpec(memory_space=pltpu.MemorySpace.SMEM),
            pl.BlockSpec(memory_space=pltpu.MemorySpace.HBM),
        ]
        + [vmem] * len(blocks),
        out_specs=[vmem] * 2,
        out_shape=[shape((8, 256, TOK), F32), shape((ENC, D))],
        scratch_shapes=[
            pltpu.VMEM((ENC, D), BF16), pltpu.VMEM((TOK, D), BF16), pltpu.SemaphoreType.DMA,
        ],
        compiler_params=pltpu.CompilerParams(vmem_limit_bytes=16 * 1024 * 1024),
        cost_estimate=pl.CostEstimate(
            flops=8 * 2 * 256 * 256 * 128, bytes_accessed=0, transcendentals=0
        ),
        name="probs",
    )(places, query, *blocks)


def body(
    resid,
    norm_gain,
    router_logits,
    router_weight,
    expert_index,
    slot,
    w_in,
    w_out,
    grad_out,
    queries,
    keys,
    values,
):
    seq = lax.axis_index("seq")
    gain = norm_gain.reshape(1, D)
    stream, upstream, query = resid[0], grad_out[0], queries[0]
    kv = jnp.concatenate([keys[0], values[0]], axis=0)
    kv_other = across(kv)
    outgoing, token_rows = call(
        dispatch_kernel,
        [stream, upstream, gain, expert_index, slot, router_logits[0].T],
        [shape((512, 768)), shape((EXPERTS + 8, TOK), F32)],
        hbm=(0, 1, 2, 3, 4, 5),
        scratch=[pltpu.VMEM((512, 768), BF16)],
        flops=2 * 512 * 512 * 768,
        limit=60,
        name="dispatch",
    )
    arrived = lax.all_to_all(outgoing, "exp", 0, 0, tiled=True)
    (block,) = call(
        collect_kernel,
        [arrived, kv, kv_other],
        [shape((208, D))],
        flops=2 * 512 * 512 * 768,
        name="collect",
    )
    block, own_in, own_out = lax.optimization_barrier((block, w_in[0].T, w_out[0]))
    other_in, other_out = across(own_in), across(own_out)
    ups, downs = [block], [block]
    for k in range(3):
        ups.append(shift(ups[-1], 1))
        downs.append(shift(downs[-1], -1))
        if k == 1:
            ups[2], downs[2], other_in = lax.optimization_barrier((ups[2], downs[2], other_in))
    weights = (own_in, own_out, other_in, other_out)
    far_in = shift(ups[3][:96], 1)
    far_grad = shift(downs[3][96:], -1)
    *near, near_kv = experts(ups + downs[1:], weights, name="experts_near")
    near, far_in = lax.optimization_barrier((near, far_in))
    own, up_parts, down_parts = near[0], near[:4], near[:1] + near[4:]
    far_a, far_b, far_kv = experts([far_in, far_grad], weights, split=True, name="experts_far")

    thirds = shift(up_parts[3], -1), shift(down_parts[3], 1)
    thirds, firsts = lax.optimization_barrier((thirds, (up_parts[1], down_parts[1])))
    back = plus(up_parts[2], thirds[0], jnp.pad(shift(far_a, -2), FIRST))
    forth = plus(down_parts[2], thirds[1], jnp.pad(shift(far_b, 2), LAST))
    sums = [own, shift(back, -2), shift(forth, 2), shift(firsts[0], -1), shift(firsts[1], 1)]

    z, y = seq % N_Z, seq // N_Z
    way = 1 - 2 * (lax.axis_index("exp") % 2)
    places = []
    for step in (0, -1, -2, -3, 1, 2, 3, 4):
        at = (z + way * step + N_Z) % N_Z
        places += [y * N_Z + at, (1 - y) * N_Z + at]
    probs, all_values = call_probs(
        jnp.stack(places).astype(jnp.int32), query, [near_kv, far_kv]
    )

    (returning,) = call(
        return_kernel,
        sums,
        [shape((512, 512))],
        scratch=[pltpu.VMEM((512, 512), BF16)],
        flops=2 * 512 * 512 * 512,
        name="return",
    )
    returned = lax.all_to_all(returning, "exp", 0, 0, tiled=True)
    grad_stream, terms = call(
        stream_kernel,
        [
            returned, token_rows, probs, all_values, router_weight.T, stream, gain, upstream, query,
        ],
        [shape((TOK, D)), shape((2048, 128))],
        hbm=(2, 3, 4, 5, 6, 7, 8),
        scratch=[pltpu.VMEM((SLOTS, WIDE), BF16)],
        flops=2 * 512 * 512 * 512 + 8 * 3 * 2 * 256 * 256 * 128,
        limit=20,
        name="stream",
    )
    terms = lax.all_to_all(terms, "seq", 0, 0, tiled=True)
    totals = jnp.sum(terms.reshape(16, 2, ENC, 128).astype(F32), axis=0).astype(BF16)
    return (grad_stream[None], totals[0][None], totals[1][None])


def solution(mesh):
    in_specs = (
        P("exp", "seq", None),
        P(),
        P("exp", "seq", None),
        P(),
        P("exp", "seq"),
        P("exp", "seq"),
        P("exp", None, "seq"),
        P("exp", "seq", None),
        P("exp", "seq", None),
        P("exp", "seq", None),
        P("exp", None, "seq"),
        P("exp", None, "seq"),
    )
    out_specs = (P("exp", "seq", None), P("exp", None, "seq"), P("exp", None, "seq"))
    return jax.shard_map(body, mesh=mesh, in_specs=in_specs, out_specs=out_specs, check_vma=False)
```

```python
import functools

import jax
import jax.numpy as jnp
from jax import lax
from jax.experimental import pallas as pl
from jax.experimental.pallas import tpu as pltpu
from jax.sharding import PartitionSpec as P

D = 2048
EXPERTS = 32
CAP = 3
SLOTS = EXPERTS * CAP
ENC = 64
TOK = 128
N_Y = 2
N_Z = 8
HID = 320
EPSILON = 1e-06
SCORE_SCALE = 0.125
COEFF = 0.7978845608
BF16 = jnp.bfloat16
F32 = jnp.float32
WIDE = D + 128


def dot(a, b, dims=((1,), (0,)), **kw):
    return lax.dot_general(a, b, (dims, ((), ())), preferred_element_type=F32, **kw)


def shuffle_matrix(parts):
    row = lax.broadcasted_iota(jnp.int32, (32 * parts, 32 * parts), 0)
    col = lax.broadcasted_iota(jnp.int32, (32 * parts, 32 * parts), 1)
    return ((row // parts == col % 32) & (row % parts == col // 32)).astype(F32).astype(BF16)


def slot_table(target):
    rows = lax.broadcasted_iota(jnp.int32, (SLOTS, TOK), 0).astype(F32)
    return (rows == target).astype(F32).astype(BF16)


def call(kernel, ins, outs, hbm=(), scratch=(), flops=0, limit=16, name=None):
    specs = [
        pl.BlockSpec(memory_space=pltpu.MemorySpace.HBM if i in hbm else pltpu.MemorySpace.VMEM)
        for i in range(len(ins))
    ]
    n = len(ins) + len(outs) + len(scratch)

    def run(*refs):
        given, held, sems = list(refs[:n]), refs[n:-1], refs[-1]
        for k, i in enumerate(hbm):
            copy = pltpu.make_async_copy(given[i], held[k], sems.at[k])
            copy.start()
            given[i] = functools.partial(arrived, copy, held[k])
        kernel(*given)

    return pl.pallas_call(
        run if hbm else kernel,
        in_specs=specs,
        out_specs=[pl.BlockSpec(memory_space=pltpu.MemorySpace.VMEM)] * len(outs),
        out_shape=outs,
        scratch_shapes=list(scratch)
        + [pltpu.VMEM(ins[i].shape, ins[i].dtype) for i in hbm]
        + ([pltpu.SemaphoreType.DMA((len(hbm),))] if hbm else []),
        compiler_params=pltpu.CompilerParams(vmem_limit_bytes=limit * 1024 * 1024),
        cost_estimate=pl.CostEstimate(flops=flops, bytes_accessed=0, transcendentals=0),
        name=name,
    )(*ins)


def arrived(copy, ref):
    copy.wait()
    return ref


def shape(dims, dtype=BF16):
    return jax.ShapeDtypeStruct(dims, dtype)


def dispatch_kernel(
    resid_ref, grad_ref, gain_ref, ids_ref, slot_ref, logits_ref, out_ref, token_ref, rows_ref
):
    stream = resid_ref()[...].astype(F32)
    root_mean = jnp.sqrt(jnp.mean(stream * stream, axis=-1, keepdims=True) + EPSILON)
    normed_in = (stream / root_mean * gain_ref()[...]).astype(BF16)
    ids, slot = ids_ref()[...], slot_ref()[...]
    target = jnp.where(slot < CAP, slot * EXPERTS + ids, -1).astype(F32)
    logits = logits_ref()[...]
    powers = jnp.exp(logits - jnp.max(logits, axis=0, keepdims=True))
    probs = powers / jnp.sum(powers, axis=0, keepdims=True)
    onehot = (lax.broadcasted_iota(jnp.int32, (EXPERTS, TOK), 0) == ids).astype(F32)
    chosen = jnp.sum(probs * onehot, axis=0, keepdims=True)
    token_ref[:EXPERTS] = chosen * (onehot - probs)
    token_ref[EXPERTS : EXPERTS + 8] = jnp.concatenate([chosen] * 4 + [target] * 4, axis=0)
    table = slot_table(target)
    for half, source in enumerate((normed_in, grad_ref()[...])):
        picked = dot(table, source).astype(BF16)
        for part in range(8):
            for c in range(CAP):
                row = (half * 8 + part) * 32
                rows_ref[row : row + 32, c * 256 : (c + 1) * 256] = picked[
                    c * 32 : (c + 1) * 32, part * 256 : (part + 1) * 256
                ]
    out_ref[...] = dot(shuffle_matrix(16), rows_ref[...]).astype(BF16)


def collect_kernel(in_ref, kv_ref, kv_other_ref, out_ref):
    rows = dot(shuffle_matrix(16), in_ref[...], ((0,), (0,))).astype(BF16)
    for half in range(2):
        for part in range(8):
            for c in range(CAP):
                row = (half * 8 + part) * 32
                out_ref[
                    half * 96 + c * 32 : half * 96 + (c + 1) * 32, part * 256 : (part + 1) * 256
                ] = rows[row : row + 32, c * 256 : (c + 1) * 256]
    for i in range(8):
        out_ref[192:208, i * 128 : (i + 1) * 128] = kv_ref[i * 16 : (i + 1) * 16, :]
        out_ref[192:208, (i + 8) * 128 : (i + 9) * 128] = kv_other_ref[i * 16 : (i + 1) * 16, :]


def expert_kernel(n, split, *refs):
    pairs, weight_refs = refs[: 2 * n], refs[2 * n : 2 * n + 4]
    out_refs, kv_ref = refs[2 * n + 4 : -1], refs[-1]
    for i, ref in enumerate(pairs[n:]):
        kv_ref[i * 16 : (i + 1) * 16] = ref[ref.shape[0] - 16 :]
    if split:
        inputs, grads = pairs[0][:96], pairs[1][:96]
    else:
        inputs = jnp.concatenate([r[:96] for r in pairs[:n]], axis=0)
        grads = jnp.concatenate([r[96:192] for r in pairs[:n]], axis=0)
    total, gate = None, None
    for k in range(2):
        w_in, w_out = weight_refs[2 * k]()[...], weight_refs[2 * k + 1]()[...]
        hidden = dot(inputs, w_in, ((1,), (1,)))
        hidden_grad = dot(grads, w_out, ((1,), (1,)))
        square = hidden * hidden
        tangent = jnp.tanh(COEFF * (hidden + 0.044715 * square * hidden))
        half = 0.5 * (1.0 + tangent)
        slope = half + 0.5 * hidden * (1.0 - tangent * tangent) * COEFF * (1.0 + 0.134145 * square)
        scaled = (hidden_grad * slope).astype(BF16)
        part = dot(scaled, w_in)
        gates = jnp.sum(half * hidden * hidden_grad, axis=1, keepdims=True)
        total = part if total is None else total + part
        gate = gates if gate is None else gate + gates
    total = total.astype(BF16)
    gate = jnp.broadcast_to(gate, (gate.shape[0], 128)).astype(BF16)
    size = 48 if split else 96
    for i, out_ref in enumerate(out_refs):
        out_ref[:, :D] = total[i * size : (i + 1) * size]
        out_ref[:, D:] = gate[i * size : (i + 1) * size]


def experts(blocks, weights, split=False, name=None):
    n = 1 if split else len(blocks)
    outs = [shape((48, WIDE))] * 2 if split else [shape((96, WIDE))] * n
    outs.append(shape((16 * n, D)))
    kernel = functools.partial(expert_kernel, n, split)
    if not split:
        kernel = lambda *refs: expert_kernel(n, False, *refs[:n], *refs[:n], *refs[n:])
    return call(
        kernel,
        list(blocks) + list(weights),
        outs,
        hbm=tuple(range(len(blocks), len(blocks) + 4)),
        flops=2 * n * 96 * D * 2 * HID * 3,
        limit=12 if split else 40,
        name=name,
    )


def return_kernel(*refs):
    parts, out_ref, rows_ref = refs[:3], refs[3], refs[4]
    total = parts[0][...].astype(F32)
    for ref in parts[1:]:
        total = total + ref[...].astype(F32)
    total = total.astype(BF16)
    rows_ref[:, 768:] = jnp.zeros((256, 128), BF16)
    for c in range(CAP):
        for part in range(8):
            rows_ref[part * 32 : (part + 1) * 32, c * 256 : (c + 1) * 256] = total[
                c * 32 : (c + 1) * 32, part * 256 : (part + 1) * 256
            ]
        rows_ref[c * 32 : (c + 1) * 32, 768:] = total[c * 32 : (c + 1) * 32, D:]
    out_ref[...] = dot(shuffle_matrix(8), rows_ref[...]).astype(BF16)


def stream_kernel(
    in_ref, token_ref, probs_ref, weight_ref, resid_ref, gain_ref, grad_ref, query_ref,
    out_ref, terms_ref, rows_ref,
):
    rows = dot(shuffle_matrix(8), in_ref[...], ((0,), (0,))).astype(BF16)
    for c in range(CAP):
        for part in range(8):
            rows_ref[c * 32 : (c + 1) * 32, part * 256 : (part + 1) * 256] = rows[
                part * 32 : (part + 1) * 32, c * 256 : (c + 1) * 256
            ]
        rows_ref[c * 32 : (c + 1) * 32, D:] = rows[c * 32 : (c + 1) * 32, 768:]
    token_ref = token_ref()
    chosen, target = token_ref[EXPERTS : EXPERTS + 1], token_ref[EXPERTS + 4 : EXPERTS + 5]
    table = slot_table(target)
    fetched = dot(table, rows_ref[:, :D], ((0,), (0,)))
    prob_grad = dot(rows_ref[:, D:], table, ((0,), (0,)))[:1]
    logit_grad = prob_grad * token_ref[:EXPERTS]
    router_term = dot(
        logit_grad, weight_ref()[...].astype(F32), ((0,), (0,)), precision=lax.Precision.HIGHEST
    )
    chosen = jnp.transpose(jnp.broadcast_to(chosen, (TOK, TOK)))[:, :1]
    stream = resid_ref()[...].astype(F32)
    root_mean = jnp.sqrt(jnp.mean(stream * stream, axis=-1, keepdims=True) + EPSILON)
    normed = stream / root_mean
    normed_grad = (chosen * fetched + router_term) * gain_ref()[...]
    mean = jnp.mean(normed_grad * normed, axis=-1, keepdims=True)
    out_ref[...] = (
        grad_ref()[...].astype(F32) + (normed_grad - normed * mean) / root_mean
    ).astype(BF16)
    attend(probs_ref(), query_ref(), out_ref, terms_ref)


def head_mask():
    row = lax.broadcasted_iota(jnp.int32, (256, 256), 0)
    col = lax.broadcasted_iota(jnp.int32, (256, 256), 1)
    return row // ENC == col // ENC


def by_head(rows, mask):
    return jnp.where(mask, jnp.concatenate([rows.astype(F32)] * 4, axis=0), 0.0).astype(BF16)


def probs_kernel(place_ref, query_ref, *refs):
    block_refs, probs_ref, values_ref, keys_ref = refs[:3], refs[3], refs[4], refs[5]
    blocks = [(r, k * 16) for r in block_refs for k in range(r.shape[0] // 16)]
    for i, (block_ref, first) in enumerate(blocks):
        for other in range(2):
            lanes = pl.ds(pl.multiple_of(place_ref[2 * i + other] * 128, 128), 128)
            for k in range(4):
                base = (other * 8 + k) * 128
                keys_ref[k * 16 : (k + 1) * 16, lanes] = block_ref[
                    first : first + 16, base : base + 128
                ]
                values_ref[k * 16 : (k + 1) * 16, lanes] = block_ref[
                    first : first + 16, base + 512 : base + 640
                ]
    mask = head_mask()
    query_ref = query_ref()
    for g in range(8):
        cols = slice(g * 256, (g + 1) * 256)
        scores = dot(by_head(keys_ref[:, cols], mask), query_ref[:, cols], ((1,), (1,)))
        scores = (scores * SCORE_SCALE).reshape(4, ENC, TOK)
        powers = jnp.exp(scores - jnp.max(scores, axis=1, keepdims=True))
        probs = powers / jnp.sum(powers, axis=1, keepdims=True)
        probs_ref[g, :256] = probs.reshape(256, TOK)
        for half in range(2):
            lanes = slice(g * 256 + half * 128, g * 256 + (half + 1) * 128)
            probs_ref[g, 256 + half * ENC : 256 + (half + 1) * ENC] = values_ref[:, lanes].astype(F32)


def attend(probs_ref, query_ref, stream_ref, out_ref):
    mask = head_mask()
    for g in range(8):
        cols = slice(g * 256, (g + 1) * 256)
        probs = probs_ref[g, :256]
        values = jnp.concatenate(
            [probs_ref[g, 256 : 256 + ENC], probs_ref[g, 256 + ENC :]], axis=1
        )
        context, query = stream_ref[:, cols], query_ref[:, cols]
        prob_grads = dot(by_head(values, mask), context, ((1,), (1,)))
        delta = jnp.sum((probs * prob_grads).reshape(4, ENC, TOK), axis=1, keepdims=True)
        delta = jnp.broadcast_to(delta, (4, ENC, TOK)).reshape(256, TOK)
        score_weights = (probs * (prob_grads - delta)).astype(BF16)
        key_terms = jnp.where(mask, dot(score_weights, query), 0.0)
        value_terms = jnp.where(mask, dot(probs.astype(BF16), context), 0.0)
        key_terms = jnp.sum(key_terms.reshape(4, ENC, 256), axis=0) * SCORE_SCALE
        value_terms = jnp.sum(value_terms.reshape(4, ENC, 256), axis=0)
        for half in range(2):
            row = (2 * g + half) * 128
            lanes = slice(half * 128, (half + 1) * 128)
            out_ref[row : row + 64] = key_terms[:, lanes].astype(BF16)
            out_ref[row + 64 : row + 128] = value_terms[:, lanes].astype(BF16)


def shift(a, step):
    pairs = []
    for y in range(N_Y):
        for z in range(N_Z):
            for e in range(EXPERTS):
                to = (z + (step if e % 2 == 0 else -step)) % N_Z
                pairs.append(((y * N_Z + z) * EXPERTS + e, (y * N_Z + to) * EXPERTS + e))
    return lax.ppermute(a, ("seq", "exp"), pairs)


def across(a):
    return lax.ppermute(a, "seq", [(s, (s + N_Z) % (N_Y * N_Z)) for s in range(N_Y * N_Z)])


FIRST, LAST = ((0, 48), (0, 0)), ((48, 0), (0, 0))


def plus(*parts):
    return functools.reduce(jnp.add, [a.astype(F32) for a in parts]).astype(BF16)


def call_probs(places, query, blocks):
    def run(place_ref, query_ref, *refs):
        held, sem = refs[-2:]
        copy = pltpu.make_async_copy(query_ref, held, sem)
        copy.start()
        probs_kernel(place_ref, functools.partial(arrived, copy, held), *refs[:-2])

    vmem = pl.BlockSpec(memory_space=pltpu.MemorySpace.VMEM)
    return pl.pallas_call(
        run,
        in_specs=[
            pl.BlockSpec(memory_space=pltpu.MemorySpace.SMEM),
            pl.BlockSpec(memory_space=pltpu.MemorySpace.HBM),
        ]
        + [vmem] * len(blocks),
        out_specs=[vmem],
        out_shape=[shape((8, 384, TOK), F32)],
        scratch_shapes=[
            pltpu.VMEM((ENC, D), BF16), pltpu.VMEM((ENC, D), BF16), pltpu.VMEM((TOK, D), BF16),
            pltpu.SemaphoreType.DMA,
        ],
        compiler_params=pltpu.CompilerParams(vmem_limit_bytes=16 * 1024 * 1024),
        cost_estimate=pl.CostEstimate(
            flops=8 * 2 * 256 * 256 * 128, bytes_accessed=0, transcendentals=0
        ),
        name="probs",
    )(places, query, *blocks)


def body(
    resid,
    norm_gain,
    router_logits,
    router_weight,
    expert_index,
    slot,
    w_in,
    w_out,
    grad_out,
    queries,
    keys,
    values,
):
    seq = lax.axis_index("seq")
    gain = norm_gain.reshape(1, D)
    stream, upstream, query = resid[0], grad_out[0], queries[0]
    kv = jnp.concatenate([keys[0], values[0]], axis=0)
    kv_other = across(kv)
    outgoing, token_rows = call(
        dispatch_kernel,
        [stream, upstream, gain, expert_index, slot, router_logits[0].T],
        [shape((512, 768)), shape((EXPERTS + 8, TOK), F32)],
        hbm=(0, 1, 2, 3, 4, 5),
        scratch=[pltpu.VMEM((512, 768), BF16)],
        flops=2 * 512 * 512 * 768,
        limit=60,
        name="dispatch",
    )
    arrived = lax.all_to_all(outgoing, "exp", 0, 0, tiled=True)
    (block,) = call(
        collect_kernel,
        [arrived, kv, kv_other],
        [shape((208, D))],
        flops=2 * 512 * 512 * 768,
        name="collect",
    )
    block, own_in, own_out = lax.optimization_barrier((block, w_in[0].T, w_out[0]))
    other_in, other_out = across(own_in), across(own_out)
    ups, downs = [block], [block]
    for k in range(3):
        ups.append(shift(ups[-1], 1))
        downs.append(shift(downs[-1], -1))
        if k == 1:
            ups[2], downs[2], other_in = lax.optimization_barrier((ups[2], downs[2], other_in))
    weights = (own_in, own_out, other_in, other_out)
    far_in = shift(ups[3][:96], 1)
    far_grad = shift(downs[3][96:], -1)
    up_3, down_3, third_kv = experts([ups[3], downs[3]], weights, name="experts_third")
    up_3, down_3, far_in = lax.optimization_barrier((up_3, down_3, far_in))
    far_a, far_b, far_kv = experts([far_in, far_grad], weights, split=True, name="experts_far")
    far_a, far_b, block = lax.optimization_barrier((far_a, far_b, block))
    *near, near_kv = experts([block, *ups[1:3], *downs[1:3]], weights, name="experts_near")
    own, up_parts, down_parts = near[0], near[:3], near[:1] + near[3:]

    back = plus(up_parts[2], shift(up_3, -1), jnp.pad(shift(far_a, -2), FIRST))
    forth = plus(down_parts[2], shift(down_3, 1), jnp.pad(shift(far_b, 2), LAST))
    back = plus(up_parts[1], shift(back, -1))
    forth = plus(down_parts[1], shift(forth, 1))
    sums = [own, shift(back, -1), shift(forth, 1)]

    z, y = seq % N_Z, seq // N_Z
    way = 1 - 2 * (lax.axis_index("exp") % 2)
    places = []
    for step in (0, -1, -2, 1, 2, -3, 3, 4):
        at = (z + way * step + N_Z) % N_Z
        places += [y * N_Z + at, (1 - y) * N_Z + at]
    (probs,) = call_probs(
        jnp.stack(places).astype(jnp.int32), query, [near_kv, third_kv, far_kv]
    )

    (returning,) = call(
        return_kernel,
        sums,
        [shape((256, 896))],
        scratch=[pltpu.VMEM((256, 896), BF16)],
        flops=2 * 256 * 256 * 896,
        name="return",
    )
    returned = lax.all_to_all(returning, "exp", 0, 0, tiled=True)
    grad_stream, terms = call(
        stream_kernel,
        [
            returned, token_rows, probs, router_weight.T, stream, gain, upstream, query,
        ],
        [shape((TOK, D)), shape((2048, 128))],
        hbm=(1, 2, 3, 4, 5, 6, 7),
        scratch=[pltpu.VMEM((SLOTS, WIDE), BF16)],
        flops=2 * 512 * 512 * 512 + 8 * 3 * 2 * 256 * 256 * 128,
        limit=20,
        name="stream",
    )
    terms = lax.all_to_all(terms, "seq", 0, 0, tiled=True)
    totals = jnp.sum(terms.reshape(16, 2, ENC, 128).astype(F32), axis=0).astype(BF16)
    return (grad_stream[None], totals[0][None], totals[1][None])


def solution(mesh):
    in_specs = (
        P("exp", "seq", None),
        P(),
        P("exp", "seq", None),
        P(),
        P("exp", "seq"),
        P("exp", "seq"),
        P("exp", None, "seq"),
        P("exp", "seq", None),
        P("exp", "seq", None),
        P("exp", "seq", None),
        P("exp", None, "seq"),
        P("exp", None, "seq"),
    )
    out_specs = (P("exp", "seq", None), P("exp", None, "seq"), P("exp", None, "seq"))
    return jax.shard_map(body, mesh=mesh, in_specs=in_specs, out_specs=out_specs, check_vma=False)
```

```python
import functools

import jax
import jax.numpy as jnp
from jax import lax
from jax.experimental import pallas as pl
from jax.experimental.pallas import tpu as pltpu
from jax.sharding import PartitionSpec as P

D = 2048
EXPERTS = 32
CAP = 3
SLOTS = EXPERTS * CAP
ENC = 64
TOK = 128
N_Y = 2
N_Z = 8
HID = 320
EPSILON = 1e-06
SCORE_SCALE = 0.125
COEFF = 0.7978845608
BF16 = jnp.bfloat16
F32 = jnp.float32
WIDE = D + 128


def dot(a, b, dims=((1,), (0,)), **kw):
    return lax.dot_general(a, b, (dims, ((), ())), preferred_element_type=F32, **kw)


def shuffle_matrix(parts):
    row = lax.broadcasted_iota(jnp.int32, (32 * parts, 32 * parts), 0)
    col = lax.broadcasted_iota(jnp.int32, (32 * parts, 32 * parts), 1)
    return ((row // parts == col % 32) & (row % parts == col // 32)).astype(F32).astype(BF16)


def slot_table(target):
    rows = lax.broadcasted_iota(jnp.int32, (SLOTS, TOK), 0).astype(F32)
    return (rows == target).astype(F32).astype(BF16)


def call(kernel, ins, outs, hbm=(), scratch=(), flops=0, limit=16, name=None):
    specs = [
        pl.BlockSpec(memory_space=pltpu.MemorySpace.HBM if i in hbm else pltpu.MemorySpace.VMEM)
        for i in range(len(ins))
    ]
    n = len(ins) + len(outs) + len(scratch)

    def run(*refs):
        given, held, sems = list(refs[:n]), refs[n:-1], refs[-1]
        for k, i in enumerate(hbm):
            copy = pltpu.make_async_copy(given[i], held[k], sems.at[k])
            copy.start()
            given[i] = functools.partial(arrived, copy, held[k])
        kernel(*given)

    return pl.pallas_call(
        run if hbm else kernel,
        in_specs=specs,
        out_specs=[pl.BlockSpec(memory_space=pltpu.MemorySpace.VMEM)] * len(outs),
        out_shape=outs,
        scratch_shapes=list(scratch)
        + [pltpu.VMEM(ins[i].shape, ins[i].dtype) for i in hbm]
        + ([pltpu.SemaphoreType.DMA((len(hbm),))] if hbm else []),
        compiler_params=pltpu.CompilerParams(vmem_limit_bytes=limit * 1024 * 1024),
        cost_estimate=pl.CostEstimate(flops=flops, bytes_accessed=0, transcendentals=0),
        name=name,
    )(*ins)


def arrived(copy, ref):
    copy.wait()
    return ref


def shape(dims, dtype=BF16):
    return jax.ShapeDtypeStruct(dims, dtype)


def dispatch_kernel(
    resid_ref, grad_ref, gain_ref, ids_ref, slot_ref, logits_ref, out_ref, token_ref, rows_ref
):
    stream = resid_ref()[...].astype(F32)
    root_mean = jnp.sqrt(jnp.mean(stream * stream, axis=-1, keepdims=True) + EPSILON)
    gain = gain_ref()[...]
    normed_in = (stream / root_mean * gain).astype(BF16)
    for i in range(16):
        token_ref[EXPERTS + 8 + i : EXPERTS + 9 + i] = gain[:, i * 128 : (i + 1) * 128]
    ids, slot = ids_ref()[...], slot_ref()[...]
    target = jnp.where(slot < CAP, slot * EXPERTS + ids, -1).astype(F32)
    logits = logits_ref()[...]
    powers = jnp.exp(logits - jnp.max(logits, axis=0, keepdims=True))
    probs = powers / jnp.sum(powers, axis=0, keepdims=True)
    onehot = (lax.broadcasted_iota(jnp.int32, (EXPERTS, TOK), 0) == ids).astype(F32)
    chosen = jnp.sum(probs * onehot, axis=0, keepdims=True)
    token_ref[:EXPERTS] = chosen * (onehot - probs)
    token_ref[EXPERTS : EXPERTS + 8] = jnp.concatenate([chosen] * 4 + [target] * 4, axis=0)
    table = slot_table(target)
    for half, source in enumerate((normed_in, grad_ref()[...])):
        picked = dot(table, source).astype(BF16)
        for part in range(8):
            for c in range(CAP):
                row = (half * 8 + part) * 32
                rows_ref[row : row + 32, c * 256 : (c + 1) * 256] = picked[
                    c * 32 : (c + 1) * 32, part * 256 : (part + 1) * 256
                ]
    out_ref[...] = dot(shuffle_matrix(16), rows_ref[...]).astype(BF16)


def collect_kernel(in_ref, kv_ref, kv_other_ref, out_ref):
    rows = dot(shuffle_matrix(16), in_ref[...], ((0,), (0,))).astype(BF16)
    for half in range(2):
        for part in range(8):
            for c in range(CAP):
                row = (half * 8 + part) * 32
                out_ref[
                    half * 96 + c * 32 : half * 96 + (c + 1) * 32, part * 256 : (part + 1) * 256
                ] = rows[row : row + 32, c * 256 : (c + 1) * 256]
    for i in range(8):
        out_ref[192:208, i * 128 : (i + 1) * 128] = kv_ref[i * 16 : (i + 1) * 16, :]
        out_ref[192:208, (i + 8) * 128 : (i + 9) * 128] = kv_other_ref[i * 16 : (i + 1) * 16, :]


def expert_kernel(n, split, *refs):
    pairs, weight_refs = refs[: 2 * n], refs[2 * n : 2 * n + 4]
    out_refs, kv_ref = refs[2 * n + 4 : -1], refs[-1]
    for i, ref in enumerate(pairs[n:]):
        kv_ref[i * 16 : (i + 1) * 16] = ref[ref.shape[0] - 16 :]
    if split:
        inputs, grads = pairs[0][:96], pairs[1][:96]
    else:
        inputs = jnp.concatenate([r[:96] for r in pairs[:n]], axis=0)
        grads = jnp.concatenate([r[96:192] for r in pairs[:n]], axis=0)
    total, gate = None, None
    for k in range(2):
        w_in, w_out = weight_refs[2 * k]()[...], weight_refs[2 * k + 1]()[...]
        hidden = dot(inputs, w_in, ((1,), (1,)))
        hidden_grad = dot(grads, w_out, ((1,), (1,)))
        square = hidden * hidden
        tangent = jnp.tanh(COEFF * (hidden + 0.044715 * square * hidden))
        half = 0.5 * (1.0 + tangent)
        slope = half + 0.5 * hidden * (1.0 - tangent * tangent) * COEFF * (1.0 + 0.134145 * square)
        scaled = (hidden_grad * slope).astype(BF16)
        part = dot(scaled, w_in)
        gates = jnp.sum(half * hidden * hidden_grad, axis=1, keepdims=True)
        total = part if total is None else total + part
        gate = gates if gate is None else gate + gates
    total = total.astype(BF16)
    gate = jnp.broadcast_to(gate, (gate.shape[0], 128)).astype(BF16)
    size = 48 if split else 96
    for i, out_ref in enumerate(out_refs):
        out_ref[:, :D] = total[i * size : (i + 1) * size]
        out_ref[:, D:] = gate[i * size : (i + 1) * size]


def experts(blocks, weights, split=False, name=None):
    n = 1 if split else len(blocks)
    outs = [shape((48, WIDE))] * 2 if split else [shape((96, WIDE))] * n
    outs.append(shape((16 * n, D)))
    kernel = functools.partial(expert_kernel, n, split)
    if not split:
        kernel = lambda *refs: expert_kernel(n, False, *refs[:n], *refs[:n], *refs[n:])
    return call(
        kernel,
        list(blocks) + list(weights),
        outs,
        hbm=tuple(range(len(blocks), len(blocks) + 4)),
        flops=2 * n * 96 * D * 2 * HID * 3,
        limit=12 if split else 40,
        name=name,
    )


def return_kernel(*refs):
    parts, out_ref, rows_ref = refs[:3], refs[3], refs[4]
    total = parts[0][...].astype(F32)
    for ref in parts[1:]:
        total = total + ref[...].astype(F32)
    total = total.astype(BF16)
    rows_ref[:, 768:] = jnp.zeros((256, 128), BF16)
    for c in range(CAP):
        for part in range(8):
            rows_ref[part * 32 : (part + 1) * 32, c * 256 : (c + 1) * 256] = total[
                c * 32 : (c + 1) * 32, part * 256 : (part + 1) * 256
            ]
        rows_ref[c * 32 : (c + 1) * 32, 768:] = total[c * 32 : (c + 1) * 32, D:]
    out_ref[...] = dot(shuffle_matrix(8), rows_ref[...]).astype(BF16)


def stream_kernel(
    in_ref, token_ref, probs_ref, weight_ref, resid_ref, grad_ref, query_ref,
    out_ref, terms_ref, rows_ref,
):
    rows = dot(shuffle_matrix(8), in_ref[...], ((0,), (0,))).astype(BF16)
    for c in range(CAP):
        for part in range(8):
            rows_ref[c * 32 : (c + 1) * 32, part * 256 : (part + 1) * 256] = rows[
                part * 32 : (part + 1) * 32, c * 256 : (c + 1) * 256
            ]
        rows_ref[c * 32 : (c + 1) * 32, D:] = rows[c * 32 : (c + 1) * 32, 768:]
    token_ref = token_ref()
    chosen, target = token_ref[EXPERTS : EXPERTS + 1], token_ref[EXPERTS + 4 : EXPERTS + 5]
    table = slot_table(target)
    fetched = dot(table, rows_ref[:, :D], ((0,), (0,)))
    prob_grad = dot(rows_ref[:, D:], table, ((0,), (0,)))[:1]
    logit_grad = prob_grad * token_ref[:EXPERTS]
    router_term = dot(
        logit_grad, weight_ref()[...].astype(F32), ((0,), (0,)), precision=lax.Precision.HIGHEST
    )
    chosen = jnp.transpose(jnp.broadcast_to(chosen, (TOK, TOK)))[:, :1]
    stream = resid_ref()[...].astype(F32)
    root_mean = jnp.sqrt(jnp.mean(stream * stream, axis=-1, keepdims=True) + EPSILON)
    normed = stream / root_mean
    gain = jnp.concatenate(
        [token_ref[EXPERTS + 8 + i : EXPERTS + 9 + i] for i in range(16)], axis=1
    )
    normed_grad = (chosen * fetched + router_term) * gain
    mean = jnp.mean(normed_grad * normed, axis=-1, keepdims=True)
    out_ref[...] = (
        grad_ref()[...].astype(F32) + (normed_grad - normed * mean) / root_mean
    ).astype(BF16)
    attend(probs_ref(), query_ref(), out_ref, terms_ref)


def head_mask():
    row = lax.broadcasted_iota(jnp.int32, (256, 256), 0)
    col = lax.broadcasted_iota(jnp.int32, (256, 256), 1)
    return row // ENC == col // ENC


def by_head(rows, mask):
    return jnp.where(mask, jnp.concatenate([rows.astype(F32)] * 4, axis=0), 0.0).astype(BF16)


def probs_kernel(place_ref, query_ref, *refs):
    block_refs, probs_ref, values_ref, keys_ref = refs[:3], refs[3], refs[4], refs[5]
    blocks = [(r, k * 16) for r in block_refs for k in range(r.shape[0] // 16)]
    for i, (block_ref, first) in enumerate(blocks):
        for other in range(2):
            lanes = pl.ds(pl.multiple_of(place_ref[2 * i + other] * 128, 128), 128)
            for k in range(4):
                base = (other * 8 + k) * 128
                keys_ref[k * 16 : (k + 1) * 16, lanes] = block_ref[
                    first : first + 16, base : base + 128
                ]
                values_ref[k * 16 : (k + 1) * 16, lanes] = block_ref[
                    first : first + 16, base + 512 : base + 640
                ]
    mask = head_mask()
    query_ref = query_ref()
    for g in range(8):
        cols = slice(g * 256, (g + 1) * 256)
        scores = dot(by_head(keys_ref[:, cols], mask), query_ref[:, cols], ((1,), (1,)))
        scores = (scores * SCORE_SCALE).reshape(4, ENC, TOK)
        powers = jnp.exp(scores - jnp.max(scores, axis=1, keepdims=True))
        probs = powers / jnp.sum(powers, axis=1, keepdims=True)
        probs_ref[g, :256] = probs.reshape(256, TOK)
        for half in range(2):
            lanes = slice(g * 256 + half * 128, g * 256 + (half + 1) * 128)
            probs_ref[g, 256 + half * ENC : 256 + (half + 1) * ENC] = values_ref[:, lanes].astype(F32)


def attend(probs_ref, query_ref, stream_ref, out_ref):
    mask = head_mask()
    for g in range(8):
        cols = slice(g * 256, (g + 1) * 256)
        probs = probs_ref[g, :256]
        values = jnp.concatenate(
            [probs_ref[g, 256 : 256 + ENC], probs_ref[g, 256 + ENC :]], axis=1
        )
        context, query = stream_ref[:, cols], query_ref[:, cols]
        prob_grads = dot(by_head(values, mask), context, ((1,), (1,)))
        delta = jnp.sum((probs * prob_grads).reshape(4, ENC, TOK), axis=1, keepdims=True)
        delta = jnp.broadcast_to(delta, (4, ENC, TOK)).reshape(256, TOK)
        score_weights = (probs * (prob_grads - delta)).astype(BF16)
        key_terms = jnp.where(mask, dot(score_weights, query), 0.0)
        value_terms = jnp.where(mask, dot(probs.astype(BF16), context), 0.0)
        key_terms = jnp.sum(key_terms.reshape(4, ENC, 256), axis=0) * SCORE_SCALE
        value_terms = jnp.sum(value_terms.reshape(4, ENC, 256), axis=0)
        for half in range(2):
            row = (2 * g + half) * 128
            lanes = slice(half * 128, (half + 1) * 128)
            out_ref[row : row + 64] = key_terms[:, lanes].astype(BF16)
            out_ref[row + 64 : row + 128] = value_terms[:, lanes].astype(BF16)


def shift(a, step):
    pairs = []
    for y in range(N_Y):
        for z in range(N_Z):
            for e in range(EXPERTS):
                to = (z + (step if e % 2 == 0 else -step)) % N_Z
                pairs.append(((y * N_Z + z) * EXPERTS + e, (y * N_Z + to) * EXPERTS + e))
    return lax.ppermute(a, ("seq", "exp"), pairs)


def across(a):
    return lax.ppermute(a, "seq", [(s, (s + N_Z) % (N_Y * N_Z)) for s in range(N_Y * N_Z)])


FIRST, LAST = ((0, 48), (0, 0)), ((48, 0), (0, 0))


def plus(*parts):
    return functools.reduce(jnp.add, [a.astype(F32) for a in parts]).astype(BF16)


def call_probs(places, query, blocks):
    def run(place_ref, query_ref, *refs):
        held, sem = refs[-2:]
        copy = pltpu.make_async_copy(query_ref, held, sem)
        copy.start()
        probs_kernel(place_ref, functools.partial(arrived, copy, held), *refs[:-2])

    vmem = pl.BlockSpec(memory_space=pltpu.MemorySpace.VMEM)
    return pl.pallas_call(
        run,
        in_specs=[
            pl.BlockSpec(memory_space=pltpu.MemorySpace.SMEM),
            pl.BlockSpec(memory_space=pltpu.MemorySpace.HBM),
        ]
        + [vmem] * len(blocks),
        out_specs=[vmem],
        out_shape=[shape((8, 384, TOK), F32)],
        scratch_shapes=[
            pltpu.VMEM((ENC, D), BF16), pltpu.VMEM((ENC, D), BF16), pltpu.VMEM((TOK, D), BF16),
            pltpu.SemaphoreType.DMA,
        ],
        compiler_params=pltpu.CompilerParams(vmem_limit_bytes=16 * 1024 * 1024),
        cost_estimate=pl.CostEstimate(
            flops=8 * 2 * 256 * 256 * 128, bytes_accessed=0, transcendentals=0
        ),
        name="probs",
    )(places, query, *blocks)


def body(
    resid,
    norm_gain,
    router_logits,
    router_weight,
    expert_index,
    slot,
    w_in,
    w_out,
    grad_out,
    queries,
    keys,
    values,
):
    seq = lax.axis_index("seq")
    gain = norm_gain.reshape(1, D)
    stream, upstream, query = resid[0], grad_out[0], queries[0]
    kv = jnp.concatenate([keys[0], values[0]], axis=0)
    kv_other = across(kv)
    outgoing, token_rows = call(
        dispatch_kernel,
        [stream, upstream, gain, expert_index, slot, router_logits[0].T],
        [shape((512, 768)), shape((EXPERTS + 24, TOK), F32)],
        hbm=(0, 1, 2, 3, 4, 5),
        scratch=[pltpu.VMEM((512, 768), BF16)],
        flops=2 * 512 * 512 * 768,
        limit=60,
        name="dispatch",
    )
    arrived = lax.all_to_all(outgoing, "exp", 0, 0, tiled=True)
    (block,) = call(
        collect_kernel,
        [arrived, kv, kv_other],
        [shape((208, D))],
        flops=2 * 512 * 512 * 768,
        name="collect",
    )
    block, own_in, own_out = lax.optimization_barrier((block, w_in[0].T, w_out[0]))
    other_in, other_out = across(own_in), across(own_out)
    ups, downs = [block], [block]
    for k in range(3):
        ups.append(shift(ups[-1], 1))
        downs.append(shift(downs[-1], -1))
        if k == 1:
            ups[2], downs[2], other_in = lax.optimization_barrier((ups[2], downs[2], other_in))
    weights = (own_in, own_out, other_in, other_out)
    far_in = shift(ups[3][:96], 1)
    far_grad = shift(downs[3][96:], -1)
    up_3, down_3, third_kv = experts([ups[3], downs[3]], weights, name="experts_third")
    up_3, down_3, far_in = lax.optimization_barrier((up_3, down_3, far_in))
    far_a, far_b, far_kv = experts([far_in, far_grad], weights, split=True, name="experts_far")
    far_a, far_b, block = lax.optimization_barrier((far_a, far_b, block))
    *near, near_kv = experts([block, *ups[1:3], *downs[1:3]], weights, name="experts_near")
    own, up_parts, down_parts = near[0], near[:3], near[:1] + near[3:]

    back = plus(up_parts[2], shift(up_3, -1), jnp.pad(shift(far_a, -2), FIRST))
    forth = plus(down_parts[2], shift(down_3, 1), jnp.pad(shift(far_b, 2), LAST))
    back = plus(up_parts[1], shift(back, -1))
    forth = plus(down_parts[1], shift(forth, 1))
    sums = [own, shift(back, -1), shift(forth, 1)]

    z, y = seq % N_Z, seq // N_Z
    way = 1 - 2 * (lax.axis_index("exp") % 2)
    places = []
    for step in (0, -1, -2, 1, 2, -3, 3, 4):
        at = (z + way * step + N_Z) % N_Z
        places += [y * N_Z + at, (1 - y) * N_Z + at]
    (probs,) = call_probs(
        jnp.stack(places).astype(jnp.int32), query, [near_kv, third_kv, far_kv]
    )

    (returning,) = call(
        return_kernel,
        sums,
        [shape((256, 896))],
        scratch=[pltpu.VMEM((256, 896), BF16)],
        flops=2 * 256 * 256 * 896,
        name="return",
    )
    returned = lax.all_to_all(returning, "exp", 0, 0, tiled=True)
    grad_stream, terms = call(
        stream_kernel,
        [
            returned, token_rows, probs, router_weight.T, stream, upstream, query,
        ],
        [shape((TOK, D)), shape((2048, 128))],
        hbm=(1, 2, 3, 4, 5, 6),
        scratch=[pltpu.VMEM((SLOTS, WIDE), BF16)],
        flops=2 * 512 * 512 * 512 + 8 * 3 * 2 * 256 * 256 * 128,
        limit=20,
        name="stream",
    )
    terms = lax.all_to_all(terms, "seq", 0, 0, tiled=True)
    totals = jnp.sum(terms.reshape(16, 2, ENC, 128).astype(F32), axis=0).astype(BF16)
    return (grad_stream[None], totals[0][None], totals[1][None])


def solution(mesh):
    in_specs = (
        P("exp", "seq", None),
        P(),
        P("exp", "seq", None),
        P(),
        P("exp", "seq"),
        P("exp", "seq"),
        P("exp", None, "seq"),
        P("exp", "seq", None),
        P("exp", "seq", None),
        P("exp", "seq", None),
        P("exp", None, "seq"),
        P("exp", None, "seq"),
    )
    out_specs = (P("exp", "seq", None), P("exp", None, "seq"), P("exp", None, "seq"))
    return jax.shard_map(body, mesh=mesh, in_specs=in_specs, out_specs=out_specs, check_vma=False)
```
